32 devices in a mesh: group: 2 (over x), dev: 16 (over z, y, core).
Axes of the slice: x: 2, y: 2, z: 4, core: 2. Of those that a mesh axis runs over, the one named last changes fastest.
Arguments:
- residual: bfloat16 [32, 8192], P(('group', 'dev')), parts along dimension 0, may hold values from -36 to 36
- queries: bfloat16 [32, 8192], P(('group', 'dev')), parts along dimension 0, may hold values from -8 to 8
- fresh_keys: bfloat16 [32, 512], P(('group', 'dev')), parts along dimension 0, may hold values from -6 to 6
- fresh_values: bfloat16 [32, 512], P(('group', 'dev')), parts along dimension 0, may hold values from -15 to 15
- key_cache: bfloat16 [32, 320, 512], P(('group', 'dev')), parts along dimension 0, may hold values from -8 to 8
- value_cache: bfloat16 [32, 320, 512], P(('group', 'dev')), parts along dimension 0, may hold values from -15 to 15
- lengths: int32 [32], P(('group', 'dev')), parts along dimension 0, may hold values from 40 to 320, as said below
- keep_inputs: int32 [32, 64], P('group'), parts along dimension 0, may hold values 0 or 1
- keep_hidden: int32 [32, 216], P('group'), parts along dimension 0, may hold values 0 or 1
- norm_gain: float32 [8192], replicated, may hold values from 0.1 to 1.9
- out_weight: bfloat16 [8192, 8192], P('dev'), may hold values from -0.0625 to 0.0625
- gate_weight: bfloat16 [27648, 8192], P('dev'), may hold values from -0.0625 to 0.0625
- up_weight: bfloat16 [27648, 8192], P('dev'), may hold values from -0.0625 to 0.0625
- down_weight: bfloat16 [27648, 8192], P('dev'), may hold values from -0.0390625 to 0.0390625
Outputs:
- post_attention: bfloat16 [32, 8192], P(('group', 'dev')), parts along dimension 0
- layer_out: bfloat16 [32, 8192], P(('group', 'dev')), parts along dimension 0
The draws below stay inside these ranges and needn't reach their ends.
There are 2 independent parts, one for each index of `group`. The reference program is written for one: setup_inputs(seed, part) draws one part's arguments, and reference() takes and returns one part's arrays. A program takes and returns all parts, laid end to end along the dimension named above; an argument that names none is the same for every part. Nothing has to cross between parts.
Inputs may be any that keep to these rules, and one draw needn't show every extreme that they name: `lengths`: some row has exactly 320 live slots.
All inputs are finite; a program needn't handle non-finite values.
Results may differ from the reference program's by a relative error of at most 0.0055.
Values may be sent and summed in bfloat16 or wider, within the bound.
A program may use at most 192 MiB of HBM per device.

```python
import math
import jax
import jax.numpy as jnp
from jax import lax

D = 8192
H = 64
KVH = 4
HD = 128
FF = 27648
BLK = 128
L = 320
ROWS = 16


def draw_queries(key, part):
    key = jax.random.fold_in(key, 11)
    entries = 1.5 * jax.random.truncated_normal(key, -5.0, 5.0, (ROWS, H * HD))
    return entries.astype(jnp.bfloat16)


def draw_key_cache(key, part):
    key = jax.random.fold_in(key, 12)
    entries = jax.random.truncated_normal(key, -5.0, 5.0, (ROWS, L, KVH * HD))
    return entries.astype(jnp.bfloat16)


def draw_lengths(key, part):
    key = jax.random.fold_in(key, 13)
    length_key, full_key = jax.random.split(key)
    drawn = jax.random.randint(length_key, (ROWS,), L // 8, L + 1)
    full_row = jax.random.randint(full_key, (), 0, ROWS)
    return jnp.where(jnp.arange(ROWS) == full_row, L, drawn).astype(jnp.int32)


def draw_residual(key, part):
    key = jax.random.fold_in(key, 14)
    row_key, column_key, base_key = jax.random.split(key, 3)
    row_scale = jnp.exp(jax.random.uniform(row_key, (ROWS, 1), minval=math.log(0.3), maxval=math.log(3.0)))
    column_scale = jnp.exp(jax.random.uniform(column_key, (1, D), minval=math.log(0.3), maxval=math.log(3.0)))
    entries = jax.random.truncated_normal(base_key, -4.0, 4.0, (ROWS, D))
    return (entries * row_scale * column_scale).astype(jnp.bfloat16)


def plant(result, stream_key, low, high):
    index_at = [jax.random.randint(jax.random.fold_in(stream_key, axis), (), 0, length) for axis, length in enumerate(result.shape)]
    main_axis = result.shape.index(max(result.shape))
    next_to = index_at[:main_axis] + [(index_at[main_axis] + 1) % result.shape[main_axis]] + index_at[main_axis + 1:]
    return result.at[tuple(index_at)].set(low).at[tuple(next_to)].set(high)


def level_of(key, dims, cuts, least, high):
    def one(axis_at, shards_of):
        heights = jax.random.uniform(jax.random.fold_in(jax.random.fold_in(key, 6), axis_at), (shards_of,), jnp.float32, least / len(cuts), high / len(cuts))
        return jnp.repeat(jnp.exp(heights), dims[axis_at] // shards_of).reshape((-1,) + (1,) * (len(dims) - axis_at - 1))

    level = one(*cuts[0])
    for cut in cuts[1:]:
        level = level * one(*cut)
    return level


def scatter_about(rng, dims, scale, most, cuts=(), held_as=jnp.bfloat16):
    values = scale * jax.random.normal(rng, dims, jnp.float32)
    if cuts:
        values = values * level_of(rng, dims, cuts, -0.22, 0.18)
    return jnp.clip(values, -most, most).astype(held_as)


def setup_inputs(seed: int = 0, part: int = 0) -> dict:
    key_list = jax.random.split(jax.random.key(seed), 15)
    part_keys = jax.random.split(jax.random.fold_in(key_list[14], part), 15)
    residual = draw_residual(jax.random.fold_in(jax.random.fold_in(key_list[14], part), 71), part)
    queries = draw_queries(jax.random.fold_in(jax.random.fold_in(key_list[14], part), 71), part)
    fresh_keys = scatter_about(part_keys[2], (ROWS, KVH * HD), 1.0, 6.0, ((0, 16),))
    fresh_values = scatter_about(part_keys[3], (ROWS, KVH * HD), 3.0, 15.0, ((0, 16),))
    key_cache = draw_key_cache(jax.random.fold_in(jax.random.fold_in(key_list[14], part), 71), part)
    value_cache = scatter_about(part_keys[5], (ROWS, L, KVH * HD), 3.0, 15.0, ((0, 16),))
    lengths = draw_lengths(jax.random.fold_in(jax.random.fold_in(key_list[14], part), 71), part)
    keep_inputs = plant((jax.random.randint(part_keys[7], (ROWS, D // BLK), 0, 2) < 1).astype(jnp.int32), jax.random.fold_in(part_keys[7], 1), 0, 1)
    keep_hidden = plant((jax.random.randint(part_keys[8], (ROWS, FF // BLK), 0, 2) < 1).astype(jnp.int32), jax.random.fold_in(part_keys[8], 1), 0, 1)
    norm_gain = jnp.clip(1.0 + 0.18 * jax.random.normal(key_list[9], (D,), jnp.float32), 0.1, 1.9)
    out_weight = scatter_about(key_list[10], (H * HD, D), (H * HD) ** -0.5, 0.0625, ((0, 16),))
    gate_weight = scatter_about(key_list[11], (FF, D), D ** -0.5, 0.0625, ((0, 16),))
    up_weight = scatter_about(key_list[12], (FF, D), D ** -0.5, 0.0625, ((0, 16),))
    down_weight = scatter_about(key_list[13], (FF, D), FF ** -0.5, 0.0390625, ((0, 16),))
    return {"residual": residual, "queries": queries, "fresh_keys": fresh_keys, "fresh_values": fresh_values, "key_cache": key_cache, "value_cache": value_cache, "lengths": lengths, "keep_inputs": keep_inputs, "keep_hidden": keep_hidden, "norm_gain": norm_gain, "out_weight": out_weight, "gate_weight": gate_weight, "up_weight": up_weight, "down_weight": down_weight}


def attend_rows(queries, fresh_keys, fresh_values, key_cache, value_cache, lengths):
    row_count = queries.shape[0]
    group_size = H // KVH
    grouped = queries.reshape(row_count, KVH, group_size, HD).astype(jnp.float32)
    key_rows = key_cache.reshape(row_count, L, KVH, HD).astype(jnp.float32)
    value_rows = value_cache.reshape(row_count, L, KVH, HD).astype(jnp.float32)
    new_keys = fresh_keys.reshape(row_count, KVH, HD).astype(jnp.float32)
    new_values = fresh_values.reshape(row_count, KVH, 1, HD).astype(jnp.float32)
    score_scale = 1.0 / math.sqrt(HD)
    cached_scores = jnp.einsum('rkgd,rlkd->rkgl', grouped, key_rows) * score_scale
    alive_mask = (jnp.arange(L)[None, :] < lengths[:, None])[:, None, None, :]
    cached_scores = jnp.where(alive_mask, cached_scores, -1e+30)
    fresh_scores = jnp.einsum('rkgd,rkd->rkg', grouped, new_keys) * score_scale
    highest = jnp.maximum(lax.optimization_barrier(jnp.max(cached_scores, axis=-1)), fresh_scores)
    cached_weights = jnp.where(alive_mask, jnp.exp(cached_scores - highest[..., None]), 0.0)
    fresh_weights = jnp.exp(fresh_scores - highest)
    totals = lax.optimization_barrier(jnp.sum(cached_weights, axis=-1)) + fresh_weights
    cached_probs = (cached_weights / totals[..., None]).astype(jnp.bfloat16)
    fresh_probs = (fresh_weights / totals).astype(jnp.bfloat16)
    blended = jnp.einsum('rkgl,rlkd->rkgd', cached_probs.astype(jnp.float32), value_rows)
    blended = blended + fresh_probs.astype(jnp.float32)[..., None] * new_values
    return blended.reshape(row_count, H * HD).astype(jnp.bfloat16)

def normalize(stream, norm_gain, keep_mask):
    row_count = stream.shape[0]
    squares = lax.optimization_barrier(jnp.mean(stream * stream, axis=-1, keepdims=True))
    scaled = stream * lax.rsqrt(squares + 1e-05) * norm_gain
    blocked = scaled.reshape(row_count, keep_mask.shape[1], -1) * keep_mask[:, :, None].astype(jnp.float32)
    return blocked.reshape(row_count, -1).astype(jnp.bfloat16)

def reference(residual, queries, fresh_keys, fresh_values, key_cache, value_cache, lengths, keep_inputs, keep_hidden, norm_gain, out_weight, gate_weight, up_weight, down_weight):
    attended = attend_rows(queries, fresh_keys, fresh_values, key_cache, value_cache, lengths)
    projected = jnp.dot(attended, out_weight, preferred_element_type=jnp.float32)
    post_attention = (residual.astype(jnp.float32) + projected).astype(jnp.bfloat16)
    ffn_input = normalize(post_attention.astype(jnp.float32), norm_gain, keep_inputs)
    gate_proj = jnp.dot(ffn_input, gate_weight.T, preferred_element_type=jnp.float32)
    up_proj = jnp.dot(ffn_input, up_weight.T, preferred_element_type=jnp.float32)
    unit_keep = jnp.repeat(keep_hidden, BLK, axis=1).astype(jnp.float32)
    activated = (jax.nn.silu(gate_proj) * up_proj * unit_keep).astype(jnp.bfloat16)
    ffn_out = jnp.dot(activated, down_weight, preferred_element_type=jnp.float32)
    layer_out = (post_attention.astype(jnp.float32) + ffn_out).astype(jnp.bfloat16)
    return (post_attention, layer_out)
```

```python
import functools
import math

import jax
import jax.numpy as jnp
from jax import lax
from jax.experimental import pallas as pl
from jax.experimental.pallas import tpu as pltpu
from jax.sharding import PartitionSpec as P

H = 64
KVH = 4
BLK = 128
LANES = 128
CHUNK = 256
MAX_SLOTS = 14
PARTS_OUT = 2
PARTS_DOWN = 4


def attend_rows(queries, fresh_keys, fresh_values, key_cache, value_cache, lengths):
    row_count, cache_span, kv_width = key_cache.shape
    head_dim = kv_width // KVH
    group_size = H // KVH
    grouped = queries.reshape(row_count, KVH, group_size, head_dim)
    key_rows = key_cache.reshape(row_count, cache_span, KVH, head_dim)
    value_rows = value_cache.reshape(row_count, cache_span, KVH, head_dim)
    score_scale = 1.0 / math.sqrt(head_dim)
    cached_scores = (
        jnp.einsum("rkgd,rlkd->rkgl", grouped, key_rows, preferred_element_type=jnp.float32)
        * score_scale
    )
    alive_mask = (jnp.arange(cache_span)[None, :] < lengths[:, None])[:, None, None, :]
    cached_scores = jnp.where(alive_mask, cached_scores, -1e30)
    fresh_scores = (
        jnp.einsum(
            "rkgd,rkd->rkg",
            grouped,
            fresh_keys.reshape(row_count, KVH, head_dim),
            preferred_element_type=jnp.float32,
        )
        * score_scale
    )
    highest = jnp.maximum(jnp.max(cached_scores, axis=-1), fresh_scores)
    cached_weights = jnp.where(alive_mask, jnp.exp(cached_scores - highest[..., None]), 0.0)
    fresh_weights = jnp.exp(fresh_scores - highest)
    totals = jnp.sum(cached_weights, axis=-1) + fresh_weights
    cached_probs = (cached_weights / totals[..., None]).astype(jnp.bfloat16)
    fresh_probs = (fresh_weights / totals).astype(jnp.bfloat16)
    blended = jnp.einsum(
        "rkgl,rlkd->rkgd", cached_probs, value_rows, preferred_element_type=jnp.float32
    )
    new_values = fresh_values.reshape(row_count, KVH, 1, head_dim).astype(jnp.float32)
    blended = blended + fresh_probs.astype(jnp.float32)[..., None] * new_values
    return blended.reshape(row_count, H * head_dim).astype(jnp.bfloat16)


def normalize(stream, norm_gain, keep_mask):
    row_count = stream.shape[0]
    squares = jnp.mean(stream * stream, axis=-1, keepdims=True)
    scaled = stream * lax.rsqrt(squares + 1e-05) * norm_gain
    blocked = scaled.reshape(row_count, keep_mask.shape[1], -1) * keep_mask[:, :, None].astype(
        jnp.float32
    )
    return blocked.reshape(row_count, -1).astype(jnp.bfloat16)


def shards(
    residual,
    queries,
    fresh_keys,
    fresh_values,
    key_cache,
    value_cache,
    lengths,
    keep_inputs,
    keep_hidden,
    norm_gain,
    out_weight,
    gate_weight,
    up_weight,
    down_weight,
):
    local_rows = residual.shape[0]
    first_row = lax.axis_index("dev") * local_rows
    attended = attend_rows(queries, fresh_keys, fresh_values, key_cache, value_cache, lengths)
    by_feature = lax.all_to_all(attended, "dev", split_axis=1, concat_axis=0, tiled=True)
    hidden_count = gate_weight.shape[0]
    unit_ids = lax.axis_index("dev") * hidden_count + jnp.arange(hidden_count)
    block_count = keep_hidden.shape[1]
    selector = (unit_ids[None, :] // BLK == jnp.arange(block_count)[:, None]).astype(jnp.float32)
    unit_keep = jnp.dot(keep_hidden.astype(jnp.float32), selector)
    contract = (((1,), (1,)), ((), ()))
    picked = by_feature
    summed = lax.psum_scatter(
        jnp.dot(picked, out_weight, preferred_element_type=jnp.float32),
        "dev",
        scatter_dimension=0,
        tiled=True,
    )
    post_attention = (residual.astype(jnp.float32) + summed).astype(jnp.bfloat16)
    keep_local = lax.dynamic_slice_in_dim(keep_inputs, first_row, local_rows, 0)
    ffn_input = normalize(post_attention.astype(jnp.float32), norm_gain, keep_local)
    inputs = lax.all_gather(ffn_input, "dev", axis=0, tiled=True)
    gate_proj = lax.dot_general(inputs, gate_weight, contract, preferred_element_type=jnp.float32)
    up_proj = lax.dot_general(inputs, up_weight, contract, preferred_element_type=jnp.float32)
    activated = (jax.nn.silu(gate_proj) * up_proj * unit_keep).astype(jnp.bfloat16)
    picked = activated
    ffn_out = lax.psum_scatter(
        jnp.dot(picked, down_weight, preferred_element_type=jnp.float32),
        "dev",
        scatter_dimension=0,
        tiled=True,
    )
    layer_out = (post_attention.astype(jnp.float32) + ffn_out).astype(jnp.bfloat16)
    return (post_attention, layer_out)


def exchange(n, me, source, target, landing, send_sem, recv_sem):
    def copy(step, where):
        return pltpu.make_async_remote_copy(
            src_ref=source(lax.rem(me + step, n)),
            dst_ref=where,
            send_sem=send_sem.at[step],
            recv_sem=recv_sem.at[step],
            device_id={"dev": lax.rem(me + step, n)},
            device_id_type=pl.DeviceIdType.MESH,
        )

    @pl.loop(1, n)
    def _(step):
        copy(step, target).start()

    def arrived(step):
        copy(step, landing(lax.rem(me + n - step, n))).wait_recv()

    def sent():
        @pl.loop(1, n)
        def _(step):
            copy(step, target).wait_send()

    return arrived, sent


def layer_kernel(
    n,
    residual,
    queries,
    fresh_keys,
    fresh_values,
    key_cache,
    value_cache,
    lengths,
    keep_inputs,
    keep_hidden,
    gain,
    out_weight,
    gate_weight,
    up_weight,
    down_weight,
    post_out,
    layer_out,
    keys,
    values,
    weights,
    stream,
    query_rows,
    feature_send,
    feature_recv,
    row_sums,
    own,
    out_send,
    out_recv,
    down_send,
    down_recv,
    gathered,
    inputs,
    activated,
    unit_keep,
    cache_sem,
    weight_sem,
    feature_ss,
    feature_rs,
    out_ss,
    out_rs,
    gather_ss,
    gather_rs,
    down_ss,
    down_rs,
):
    me = lax.axis_index("dev")
    width = residual.shape[1]
    pieces = width // LANES
    head_dim = LANES
    group_size = H // KVH
    heads_here = H // n
    cache_span = key_cache.shape[1]
    hidden = gate_weight.shape[0]
    starts = list(range(0, hidden, CHUNK))
    sizes = [min(CHUNK, hidden - at) for at in starts]
    count = len(starts)
    out_rows = out_weight.shape[0]
    out_count = out_rows // CHUNK
    bf16, f32 = jnp.bfloat16, jnp.float32

    barrier = pltpu.get_barrier_semaphore()

    @pl.loop(1, n)
    def _(step):
        pl.semaphore_signal(
            barrier,
            inc=1,
            device_id={"dev": lax.rem(me + step, n)},
            device_id_type=pl.DeviceIdType.MESH,
        )

    def fetch(array, at, size, slot, sem):
        return pltpu.make_async_copy(
            array.at[pl.ds(at, size)], weights.at[slot, pl.ds(0, size)], weight_sem.at[sem]
        )

    key_copy = pltpu.make_async_copy(key_cache.at[0], keys, cache_sem.at[0])
    value_copy = pltpu.make_async_copy(value_cache.at[0], values, cache_sem.at[1])
    key_copy.start()
    value_copy.start()
    out_first = 2 * (count - 1)
    out_copies = [
        fetch(out_weight, i * CHUNK, CHUNK, out_first + i, i) for i in range(out_count)
    ]
    gate_copies, up_copies, down_copies = [], [], []
    for i in range(count):
        sem = out_count + 3 * i
        gate_copies.append(fetch(gate_weight, starts[i], sizes[i], 2 * i, sem))
        up_copies.append(fetch(up_weight, starts[i], sizes[i], 2 * i + 1, sem + 1))
        down_copies.append(fetch(down_weight, starts[i], sizes[i], i, sem + 2))
    for copy in out_copies:
        copy.start()
    for i in range(count - 1):
        gate_copies[i].start()
        up_copies[i].start()

    query_row = queries[...].astype(f32)
    residual_row = residual[...].astype(f32)
    for c in range(pieces):
        lanes = slice(c * LANES, (c + 1) * LANES)
        query_rows[c : c + 1, :] = query_row[:, lanes]
        stream[c : c + 1, :] = residual_row[:, lanes]

    key_copy.wait()
    value_copy.wait()
    scale = 1.0 / math.sqrt(head_dim)
    alive = lax.broadcasted_iota(jnp.int32, (group_size, cache_span), 1) < lengths[0]
    by_lane = (((1,), (1,)), ((), ()))
    for k in range(KVH):
        lanes = slice(k * head_dim, (k + 1) * head_dim)
        query = query_rows[k * group_size : (k + 1) * group_size, :]
        scores = (
            lax.dot_general(
                query.astype(bf16), keys[:, lanes], by_lane, preferred_element_type=f32
            )
            * scale
        )
        scores = jnp.where(alive, scores, -1e30)
        fresh = (
            jnp.sum(query * fresh_keys[:, lanes].astype(f32), axis=1, keepdims=True) * scale
        )
        highest = jnp.maximum(jnp.max(scores, axis=1, keepdims=True), fresh)
        cached_weights = jnp.where(alive, jnp.exp(scores - highest), 0.0)
        fresh_weights = jnp.exp(fresh - highest)
        totals = jnp.sum(cached_weights, axis=1, keepdims=True) + fresh_weights
        probs = (cached_weights / totals).astype(bf16)
        fresh_probs = (fresh_weights / totals).astype(bf16).astype(f32)
        blended = jnp.dot(probs, values[:, lanes], preferred_element_type=f32)
        blended = blended + fresh_probs * fresh_values[:, lanes].astype(f32)
        blended = blended.astype(bf16).astype(f32)
        for at in range(0, group_size, heads_here):
            feature_send[(k * group_size + at) // heads_here] = blended[at : at + heads_here]

    pl.semaphore_wait(barrier, n - 1)
    arrived, features_sent = exchange(
        n,
        me,
        lambda peer: feature_send.at[peer],
        feature_recv.at[me],
        lambda peer: feature_recv.at[peer],
        feature_ss,
        feature_rs,
    )
    feature_recv[pl.ds(me, 1)] = feature_send[pl.ds(me, 1)]

    blocks = keep_hidden.shape[1]
    unit = me * hidden + lax.broadcasted_iota(jnp.int32, (blocks, hidden), 1)
    first = BLK * lax.broadcasted_iota(jnp.int32, (blocks, hidden), 0)
    selector = jnp.where((unit >= first) & (unit < first + BLK), 1.0, 0.0).astype(bf16)
    unit_keep[...] = jnp.dot(
        keep_hidden[...].astype(f32).astype(bf16), selector, preferred_element_type=f32
    )

    for copy in out_copies:
        copy.wait()

    @pl.loop(1, n)
    def _(step):
        arrived(step)

    def send_sums(part, parts, product, send, recv, send_sem, recv_sem):
        rows = pieces // parts
        for c in range(rows):
            row_sums[:, part * rows + c, :] = product[:, c * LANES : (c + 1) * LANES]
        here = pl.ds(part * rows, rows)

        @pl.loop(0, n)
        def _(r):
            send[part, r] = row_sums[r, here].astype(bf16)

        started = exchange(
            n,
            me,
            lambda peer: send.at[part, peer],
            recv.at[part, me],
            lambda peer: recv.at[part, peer],
            send_sem.at[part],
            recv_sem.at[part],
        )
        own[here] = row_sums[me, here]
        return started

    def add_sums(part, parts, started, recv):
        rows = pieces // parts
        here = pl.ds(part * rows, rows)

        def add(step, total):
            started[0](step)
            return total + recv[part, lax.rem(me + n - step, n)].astype(f32)

        total = lax.fori_loop(1, n, add, own[here])
        return total

    features = jnp.concatenate(
        [feature_recv[:, h, :].astype(bf16) for h in range(heads_here)], axis=1
    )
    out_started = []
    part_width = width // PARTS_OUT
    for part in range(PARTS_OUT):
        columns = slice(part * part_width, (part + 1) * part_width)
        product = None
        for i in range(out_count):
            term = jnp.dot(
                features[:, i * CHUNK : (i + 1) * CHUNK],
                weights[out_first + i, :, columns],
                preferred_element_type=f32,
            )
            product = term if product is None else product + term
        out_started.append(
            send_sums(part, PARTS_OUT, product, out_send, out_recv, out_ss, out_rs)
        )
    gate_copies[count - 1].start()
    up_copies[count - 1].start()
    for part in range(PARTS_OUT):
        rows = pieces // PARTS_OUT
        here = pl.ds(part * rows, rows)
        total = add_sums(part, PARTS_OUT, out_started[part], out_recv)
        stream[here] = (stream[here] + total).astype(bf16).astype(f32)

    post = stream[...]
    squares = jnp.sum(jnp.sum(post * post, axis=1, keepdims=True), axis=0, keepdims=True) / width
    mask_row = jnp.broadcast_to(keep_inputs[pl.ds(me, 1), :].astype(f32), (pieces, pieces))
    diagonal = lax.broadcasted_iota(jnp.int32, (pieces, pieces), 0) == lax.broadcasted_iota(
        jnp.int32, (pieces, pieces), 1
    )
    mask = jnp.sum(jnp.where(diagonal, mask_row, 0.0), axis=1, keepdims=True)
    scaled = post * lax.rsqrt(squares + 1e-05) * gain[...] * mask
    gathered[me] = scaled.astype(bf16)
    arrived, inputs_sent = exchange(
        n,
        me,
        lambda peer: gathered.at[me],
        gathered.at[me],
        lambda peer: gathered.at[peer],
        gather_ss,
        gather_rs,
    )
    for c in range(pieces):
        post_out[:, c * LANES : (c + 1) * LANES] = stream[c : c + 1, :].astype(bf16)
    row_sums[me] = scaled.astype(bf16).astype(f32)

    @pl.loop(1, n)
    def _(step):
        arrived(step)
        peer = lax.rem(me + n - step, n)
        row_sums[peer] = gathered[peer].astype(f32)

    for c in range(pieces):
        inputs[:, c * LANES : (c + 1) * LANES] = row_sums[:, c, :].astype(bf16)

    for i in range(count):
        gate_copies[i].wait()
        up_copies[i].wait()
        units = slice(starts[i], starts[i] + sizes[i])
        gate = lax.dot_general(
            inputs[...], weights[2 * i, 0 : sizes[i], :], by_lane, preferred_element_type=f32
        )
        up = lax.dot_general(
            inputs[...], weights[2 * i + 1, 0 : sizes[i], :], by_lane, preferred_element_type=f32
        )
        silu = gate / (1.0 + jnp.exp(-gate))
        activated[:, units] = (silu * up * unit_keep[:, units]).astype(bf16)
        for j in (2 * i, 2 * i + 1):
            if j < count:
                down_copies[j].start()

    for copy in down_copies:
        copy.wait()
    down_started = []
    part_width = width // PARTS_DOWN
    for part in range(PARTS_DOWN):
        columns = slice(part * part_width, (part + 1) * part_width)
        product = None
        for i in range(count):
            term = jnp.dot(
                activated[:, starts[i] : starts[i] + sizes[i]],
                weights[i, 0 : sizes[i], columns],
                preferred_element_type=f32,
            )
            product = term if product is None else product + term
        down_started.append(
            send_sums(part, PARTS_DOWN, product, down_send, down_recv, down_ss, down_rs)
        )
    for part in range(PARTS_DOWN):
        rows = pieces // PARTS_DOWN
        here = pl.ds(part * rows, rows)
        total = add_sums(part, PARTS_DOWN, down_started[part], down_recv)
        stream[here] = stream[here] + total
    for c in range(pieces):
        layer_out[:, c * LANES : (c + 1) * LANES] = stream[c : c + 1, :].astype(bf16)

    features_sent()
    inputs_sent()
    for started in out_started + down_started:
        started[1]()


def fused_layer(n, *operands):
    (
        residual,
        _,
        _,
        _,
        key_cache,
        _,
        _,
        keep_inputs,
        keep_hidden,
        norm_gain,
        out_weight,
        gate_weight,
        _,
        _,
    ) = operands
    width = residual.shape[1]
    pieces = width // LANES
    hidden = gate_weight.shape[0]
    count = -(-hidden // CHUNK)
    slots = 2 * count
    bf16, f32 = jnp.bfloat16, jnp.float32
    dma = pltpu.SemaphoreType.DMA
    vmem = pl.BlockSpec(memory_space=pltpu.VMEM)
    smem = pl.BlockSpec(memory_space=pltpu.SMEM)
    hbm = pl.BlockSpec(memory_space=pl.ANY)
    operands = list(operands)
    operands[9] = norm_gain.reshape(pieces, LANES)
    cache_shape = key_cache.shape[1:]
    row_shape = jax.ShapeDtypeStruct(residual.shape, bf16)
    weight_bytes = 2 * (out_weight.size + 3 * gate_weight.size)
    return pl.pallas_call(
        functools.partial(layer_kernel, n),
        out_shape=(row_shape, row_shape),
        in_specs=[vmem] * 4 + [hbm] * 2 + [smem] + [vmem] * 3 + [hbm] * 4,
        out_specs=(vmem, vmem),
        scratch_shapes=[
            pltpu.VMEM(cache_shape, bf16),
            pltpu.VMEM(cache_shape, bf16),
            pltpu.VMEM((slots, CHUNK, width), bf16),
            pltpu.VMEM((pieces, LANES), f32),
            pltpu.VMEM((pieces, LANES), f32),
            pltpu.VMEM((n, H // n, LANES), f32),
            pltpu.VMEM((n, H // n, LANES), f32),
            pltpu.VMEM((n, pieces, LANES), f32),
            pltpu.VMEM((pieces, LANES), f32),
            pltpu.VMEM((PARTS_OUT, n, pieces // PARTS_OUT, LANES), bf16),
            pltpu.VMEM((PARTS_OUT, n, pieces // PARTS_OUT, LANES), bf16),
            pltpu.VMEM((PARTS_DOWN, n, pieces // PARTS_DOWN, LANES), bf16),
            pltpu.VMEM((PARTS_DOWN, n, pieces // PARTS_DOWN, LANES), bf16),
            pltpu.VMEM((n, pieces, LANES), bf16),
            pltpu.VMEM((n, width), bf16),
            pltpu.VMEM((n, hidden), bf16),
            pltpu.VMEM((n, hidden), f32),
            dma((2,)),
            dma((out_weight.shape[0] // CHUNK + 3 * count,)),
            dma((n,)),
            dma((n,)),
            dma((PARTS_OUT, n)),
            dma((PARTS_OUT, n)),
            dma((n,)),
            dma((n,)),
            dma((PARTS_DOWN, n)),
            dma((PARTS_DOWN, n)),
        ],
        compiler_params=pltpu.CompilerParams(
            collective_id=0, has_side_effects=True, vmem_limit_bytes=63 * 2**20
        ),
        cost_estimate=pl.CostEstimate(
            flops=n * weight_bytes, bytes_accessed=weight_bytes, transcendentals=0
        ),
        name="layer",
    )(*operands)


def one_row_each(n, *operands):
    residual, gate_weight, out_weight = operands[0], operands[11], operands[10]
    slots = 2 * -(-gate_weight.shape[0] // CHUNK)
    return (
        residual.shape[0] == 1
        and n % 16 == 0
        and (H // KVH) % max(H // n, 1) == 0
        and out_weight.shape[0] == (H // n) * LANES
        and out_weight.shape[0] == 2 * CHUNK
        and 2 < slots <= MAX_SLOTS
        and gate_weight.shape[0] % 64 == 0
    )


def layer(n, *operands):
    if one_row_each(n, *operands):
        return fused_layer(n, *operands)
    return shards(*operands)


def solution(mesh):
    in_specs = (
        P(("group", "dev"), None),
        P(("group", "dev"), None),
        P(("group", "dev"), None),
        P(("group", "dev"), None),
        P(("group", "dev"), None, None),
        P(("group", "dev"), None, None),
        P(("group", "dev")),
        P("group", None),
        P("group", None),
        P(),
        P("dev", None),
        P("dev", None),
        P("dev", None),
        P("dev", None),
    )
    out_specs = (P(("group", "dev"), None), P(("group", "dev"), None))
    body = functools.partial(layer, mesh.shape["dev"])
    return jax.shard_map(body, mesh=mesh, in_specs=in_specs, out_specs=out_specs, check_vma=False)
```

```python
import functools
import math

import jax
import jax.numpy as jnp
from jax import lax
from jax.experimental import pallas as pl
from jax.experimental.pallas import tpu as pltpu
from jax.sharding import PartitionSpec as P

H = 64
KVH = 4
BLK = 128
LANES = 128
CHUNK = 256
MAX_SLOTS = 14
PARTS_OUT = 2
PARTS_DOWN = 4


def attend_rows(queries, fresh_keys, fresh_values, key_cache, value_cache, lengths):
    row_count, cache_span, kv_width = key_cache.shape
    head_dim = kv_width // KVH
    group_size = H // KVH
    grouped = queries.reshape(row_count, KVH, group_size, head_dim)
    key_rows = key_cache.reshape(row_count, cache_span, KVH, head_dim)
    value_rows = value_cache.reshape(row_count, cache_span, KVH, head_dim)
    score_scale = 1.0 / math.sqrt(head_dim)
    cached_scores = (
        jnp.einsum("rkgd,rlkd->rkgl", grouped, key_rows, preferred_element_type=jnp.float32)
        * score_scale
    )
    alive_mask = (jnp.arange(cache_span)[None, :] < lengths[:, None])[:, None, None, :]
    cached_scores = jnp.where(alive_mask, cached_scores, -1e30)
    fresh_scores = (
        jnp.einsum(
            "rkgd,rkd->rkg",
            grouped,
            fresh_keys.reshape(row_count, KVH, head_dim),
            preferred_element_type=jnp.float32,
        )
        * score_scale
    )
    highest = jnp.maximum(jnp.max(cached_scores, axis=-1), fresh_scores)
    cached_weights = jnp.where(alive_mask, jnp.exp(cached_scores - highest[..., None]), 0.0)
    fresh_weights = jnp.exp(fresh_scores - highest)
    totals = jnp.sum(cached_weights, axis=-1) + fresh_weights
    cached_probs = (cached_weights / totals[..., None]).astype(jnp.bfloat16)
    fresh_probs = (fresh_weights / totals).astype(jnp.bfloat16)
    blended = jnp.einsum(
        "rkgl,rlkd->rkgd", cached_probs, value_rows, preferred_element_type=jnp.float32
    )
    new_values = fresh_values.reshape(row_count, KVH, 1, head_dim).astype(jnp.float32)
    blended = blended + fresh_probs.astype(jnp.float32)[..., None] * new_values
    return blended.reshape(row_count, H * head_dim).astype(jnp.bfloat16)


def normalize(stream, norm_gain, keep_mask):
    row_count = stream.shape[0]
    squares = jnp.mean(stream * stream, axis=-1, keepdims=True)
    scaled = stream * lax.rsqrt(squares + 1e-05) * norm_gain
    blocked = scaled.reshape(row_count, keep_mask.shape[1], -1) * keep_mask[:, :, None].astype(
        jnp.float32
    )
    return blocked.reshape(row_count, -1).astype(jnp.bfloat16)


def shards(
    residual,
    queries,
    fresh_keys,
    fresh_values,
    key_cache,
    value_cache,
    lengths,
    keep_inputs,
    keep_hidden,
    norm_gain,
    out_weight,
    gate_weight,
    up_weight,
    down_weight,
):
    local_rows = residual.shape[0]
    first_row = lax.axis_index("dev") * local_rows
    attended = attend_rows(queries, fresh_keys, fresh_values, key_cache, value_cache, lengths)
    by_feature = lax.all_to_all(attended, "dev", split_axis=1, concat_axis=0, tiled=True)
    hidden_count = gate_weight.shape[0]
    unit_ids = lax.axis_index("dev") * hidden_count + jnp.arange(hidden_count)
    block_count = keep_hidden.shape[1]
    selector = (unit_ids[None, :] // BLK == jnp.arange(block_count)[:, None]).astype(jnp.float32)
    unit_keep = jnp.dot(keep_hidden.astype(jnp.float32), selector)
    contract = (((1,), (1,)), ((), ()))
    picked = by_feature
    summed = lax.psum_scatter(
        jnp.dot(picked, out_weight, preferred_element_type=jnp.float32),
        "dev",
        scatter_dimension=0,
        tiled=True,
    )
    post_attention = (residual.astype(jnp.float32) + summed).astype(jnp.bfloat16)
    keep_local = lax.dynamic_slice_in_dim(keep_inputs, first_row, local_rows, 0)
    ffn_input = normalize(post_attention.astype(jnp.float32), norm_gain, keep_local)
    inputs = lax.all_gather(ffn_input, "dev", axis=0, tiled=True)
    gate_proj = lax.dot_general(inputs, gate_weight, contract, preferred_element_type=jnp.float32)
    up_proj = lax.dot_general(inputs, up_weight, contract, preferred_element_type=jnp.float32)
    activated = (jax.nn.silu(gate_proj) * up_proj * unit_keep).astype(jnp.bfloat16)
    picked = activated
    ffn_out = lax.psum_scatter(
        jnp.dot(picked, down_weight, preferred_element_type=jnp.float32),
        "dev",
        scatter_dimension=0,
        tiled=True,
    )
    layer_out = (post_attention.astype(jnp.float32) + ffn_out).astype(jnp.bfloat16)
    return (post_attention, layer_out)


def exchange(count, to, source, target, landing, send_sem, recv_sem):
    def copy(step, where):
        return pltpu.make_async_remote_copy(
            src_ref=source(step),
            dst_ref=where,
            send_sem=send_sem.at[step],
            recv_sem=recv_sem.at[step],
            device_id={"dev": to(step)},
            device_id_type=pl.DeviceIdType.MESH,
        )

    @pl.loop(1, count)
    def _(step):
        copy(step, target).start()

    def arrived(step):
        copy(step, landing(step)).wait_recv()

    def sent():
        @pl.loop(1, count)
        def _(step):
            copy(step, target).wait_send()

    return arrived, sent


def layer_kernel(
    n,
    residual,
    queries,
    fresh_keys,
    fresh_values,
    key_cache,
    value_cache,
    lengths,
    keep_inputs,
    keep_hidden,
    gain,
    out_weight,
    gate_weight,
    up_weight,
    down_weight,
    post_out,
    layer_out,
    keys,
    values,
    weights,
    stream,
    query_rows,
    feature_send,
    feature_recv,
    row_sums,
    own,
    out_near,
    out_far,
    down_near,
    down_far,
    gathered,
    inputs,
    activated,
    unit_keep,
    cache_sem,
    weight_sem,
    feature_ss,
    feature_rs,
    out_ss,
    out_rs,
    gather_ss,
    gather_rs,
    relay_ss,
    relay_rs,
    down_ss,
    down_rs,
):
    me = lax.axis_index("dev")
    pairs = n // 2
    pair, side = me // 2, lax.rem(me, 2)
    partner = me + 1 - 2 * side

    def pair_to(step):
        return lax.rem(pair + step, pairs)

    def pair_from(step):
        return lax.rem(pair + pairs - step, pairs)

    width = residual.shape[1]
    pieces = width // LANES
    head_dim = LANES
    group_size = H // KVH
    heads_here = H // n
    cache_span = key_cache.shape[1]
    hidden = gate_weight.shape[0]
    starts = list(range(0, hidden, CHUNK))
    sizes = [min(CHUNK, hidden - at) for at in starts]
    count = len(starts)
    out_rows = out_weight.shape[0]
    out_count = out_rows // CHUNK
    bf16, f32 = jnp.bfloat16, jnp.float32

    barrier = pltpu.get_barrier_semaphore()

    @pl.loop(1, n)
    def _(step):
        pl.semaphore_signal(
            barrier,
            inc=1,
            device_id={"dev": lax.rem(me + step, n)},
            device_id_type=pl.DeviceIdType.MESH,
        )

    def fetch(array, at, size, slot, sem):
        return pltpu.make_async_copy(
            array.at[pl.ds(at, size)], weights.at[slot, pl.ds(0, size)], weight_sem.at[sem]
        )

    key_copy = pltpu.make_async_copy(key_cache.at[0], keys, cache_sem.at[0])
    value_copy = pltpu.make_async_copy(value_cache.at[0], values, cache_sem.at[1])
    key_copy.start()
    value_copy.start()
    out_first = 2 * (count - 1)
    out_copies = [
        fetch(out_weight, i * CHUNK, CHUNK, out_first + i, i) for i in range(out_count)
    ]
    gate_copies, up_copies, down_copies = [], [], []
    for i in range(count):
        sem = out_count + 3 * i
        gate_copies.append(fetch(gate_weight, starts[i], sizes[i], 2 * i, sem))
        up_copies.append(fetch(up_weight, starts[i], sizes[i], 2 * i + 1, sem + 1))
        down_copies.append(fetch(down_weight, starts[i], sizes[i], i, sem + 2))
    for copy in out_copies:
        copy.start()
    for i in range(count - 1):
        gate_copies[i].start(priority=1)
        up_copies[i].start(priority=1)

    query_row = queries[...].astype(f32)
    residual_row = residual[...].astype(f32)
    for c in range(pieces):
        lanes = slice(c * LANES, (c + 1) * LANES)
        query_rows[c : c + 1, :] = query_row[:, lanes]
        stream[c : c + 1, :] = residual_row[:, lanes]

    key_copy.wait()
    value_copy.wait()
    scale = 1.0 / math.sqrt(head_dim)
    alive = lax.broadcasted_iota(jnp.int32, (group_size, cache_span), 1) < lengths[0]
    by_lane = (((1,), (1,)), ((), ()))
    for k in range(KVH):
        lanes = slice(k * head_dim, (k + 1) * head_dim)
        query = query_rows[k * group_size : (k + 1) * group_size, :]
        scores = (
            lax.dot_general(
                query.astype(bf16), keys[:, lanes], by_lane, preferred_element_type=f32
            )
            * scale
        )
        scores = jnp.where(alive, scores, -1e30)
        fresh = (
            jnp.sum(query * fresh_keys[:, lanes].astype(f32), axis=1, keepdims=True) * scale
        )
        highest = jnp.maximum(jnp.max(scores, axis=1, keepdims=True), fresh)
        cached_weights = jnp.where(alive, jnp.exp(scores - highest), 0.0)
        fresh_weights = jnp.exp(fresh - highest)
        totals = jnp.sum(cached_weights, axis=1, keepdims=True) + fresh_weights
        probs = (cached_weights / totals).astype(bf16)
        fresh_probs = (fresh_weights / totals).astype(bf16).astype(f32)
        blended = jnp.dot(probs, values[:, lanes], preferred_element_type=f32)
        blended = blended + fresh_probs * fresh_values[:, lanes].astype(f32)
        blended = blended.astype(bf16).astype(f32)
        for at in range(0, group_size, heads_here):
            feature_send[(k * group_size + at) // heads_here] = blended[at : at + heads_here]

    pl.semaphore_wait(barrier, n - 1)
    arrived, features_sent = exchange(
        n,
        lambda step: lax.rem(me + step, n),
        lambda step: feature_send.at[lax.rem(me + step, n)],
        feature_recv.at[me],
        lambda step: feature_recv.at[lax.rem(me + n - step, n)],
        feature_ss,
        feature_rs,
    )
    feature_recv[pl.ds(me, 1)] = feature_send[pl.ds(me, 1)]

    blocks = keep_hidden.shape[1]
    unit = me * hidden + lax.broadcasted_iota(jnp.int32, (blocks, hidden), 1)
    first = BLK * lax.broadcasted_iota(jnp.int32, (blocks, hidden), 0)
    selector = jnp.where((unit >= first) & (unit < first + BLK), 1.0, 0.0).astype(bf16)
    unit_keep[...] = jnp.dot(
        keep_hidden[...].astype(f32).astype(bf16), selector, preferred_element_type=f32
    )

    for copy in out_copies:
        copy.wait()

    @pl.loop(1, n)
    def _(step):
        arrived(step)

    def pair_copy(part, near, sems):
        return pltpu.make_async_remote_copy(
            src_ref=near.at[0, part],
            dst_ref=near.at[1, part],
            send_sem=sems[0].at[part, 0],
            recv_sem=sems[1].at[part, 0],
            device_id={"dev": partner},
            device_id_type=pl.DeviceIdType.MESH,
        )

    def to_partner(part, parts, product, near, sems):
        rows = pieces // parts
        here = pl.ds(part * rows, rows)
        for c in range(rows):
            row_sums[:, part * rows + c, :] = product[:, c * LANES : (c + 1) * LANES]

        @pl.loop(0, pairs)
        def _(r):
            near[0, part, r] = row_sums[2 * r + 1 - side, here].astype(bf16)

        pair_copy(part, near, sems).start()

    def to_owners(part, parts, near, far, sems):
        rows = pieces // parts
        here = pl.ds(part * rows, rows)
        pair_copy(part, near, sems).wait_recv()

        @pl.loop(0, pairs)
        def _(r):
            both = row_sums[2 * r + side, here] + near[1, part, r].astype(f32)
            far[0, part, r] = both.astype(bf16)

        started = exchange(
            pairs,
            lambda step: 2 * pair_to(step) + side,
            lambda step: far.at[0, part, pair_to(step)],
            far.at[1, part, pair],
            lambda step: far.at[1, part, pair_from(step)],
            sems[0].at[part],
            sems[1].at[part],
        )
        own[here] = row_sums[me, here] + near[1, part, pair].astype(f32)
        return started

    def add_sums(part, parts, started, far):
        rows = pieces // parts
        here = pl.ds(part * rows, rows)

        def add(step, total):
            started[0](step)
            return total + far[1, part, pair_from(step)].astype(f32)

        return lax.fori_loop(1, pairs, add, own[here])

    features = jnp.concatenate(
        [feature_recv[:, h, :].astype(bf16) for h in range(heads_here)], axis=1
    )
    out_started = []
    out_sems, down_sems = (out_ss, out_rs), (down_ss, down_rs)
    part_width = width // PARTS_OUT
    for part in range(PARTS_OUT):
        columns = slice(part * part_width, (part + 1) * part_width)
        product = None
        for i in range(out_count):
            term = jnp.dot(
                features[:, i * CHUNK : (i + 1) * CHUNK],
                weights[out_first + i, :, columns],
                preferred_element_type=f32,
            )
            product = term if product is None else product + term
        to_partner(part, PARTS_OUT, product, out_near, out_sems)
    gate_copies[count - 1].start(priority=1)
    up_copies[count - 1].start(priority=1)
    for part in range(PARTS_OUT):
        out_started.append(to_owners(part, PARTS_OUT, out_near, out_far, out_sems))
    for part in range(PARTS_OUT):
        rows = pieces // PARTS_OUT
        here = pl.ds(part * rows, rows)
        total = add_sums(part, PARTS_OUT, out_started[part], out_far)
        stream[here] = (stream[here] + total).astype(bf16).astype(f32)

    post = stream[...]
    squares = jnp.sum(jnp.sum(post * post, axis=1, keepdims=True), axis=0, keepdims=True) / width
    mask_row = jnp.broadcast_to(keep_inputs[pl.ds(me, 1), :].astype(f32), (pieces, pieces))
    diagonal = lax.broadcasted_iota(jnp.int32, (pieces, pieces), 0) == lax.broadcasted_iota(
        jnp.int32, (pieces, pieces), 1
    )
    mask = jnp.sum(jnp.where(diagonal, mask_row, 0.0), axis=1, keepdims=True)
    scaled = post * lax.rsqrt(squares + 1e-05) * gain[...] * mask
    gathered[me] = scaled.astype(bf16)
    arrived, inputs_sent = exchange(
        pairs,
        lambda step: 2 * pair_to(step) + side,
        lambda step: gathered.at[me],
        gathered.at[me],
        lambda step: gathered.at[2 * pair_from(step) + side],
        gather_ss,
        gather_rs,
    )

    def relay(step, row):
        return pltpu.make_async_remote_copy(
            src_ref=gathered.at[2 * pair_from(step) + side],
            dst_ref=gathered.at[row],
            send_sem=relay_ss.at[step],
            recv_sem=relay_rs.at[step],
            device_id={"dev": partner},
            device_id_type=pl.DeviceIdType.MESH,
        )

    relay(0, me).start()
    for c in range(pieces):
        post_out[:, c * LANES : (c + 1) * LANES] = stream[c : c + 1, :].astype(bf16)
    row_sums[me] = scaled.astype(bf16).astype(f32)

    @pl.loop(1, pairs)
    def _(step):
        arrived(step)
        row = 2 * pair_from(step) + side
        relay(step, row).start()
        row_sums[row] = gathered[row].astype(f32)

    @pl.loop(0, pairs)
    def _(step):
        row = 2 * pair_from(step) + 1 - side
        relay(step, row).wait_recv()
        row_sums[row] = gathered[row].astype(f32)

    for c in range(pieces):
        inputs[:, c * LANES : (c + 1) * LANES] = row_sums[:, c, :].astype(bf16)

    for i in range(count):
        gate_copies[i].wait()
        up_copies[i].wait()
        units = slice(starts[i], starts[i] + sizes[i])
        gate = lax.dot_general(
            inputs[...], weights[2 * i, 0 : sizes[i], :], by_lane, preferred_element_type=f32
        )
        up = lax.dot_general(
            inputs[...], weights[2 * i + 1, 0 : sizes[i], :], by_lane, preferred_element_type=f32
        )
        silu = gate / (1.0 + jnp.exp(-gate))
        activated[:, units] = (silu * up * unit_keep[:, units]).astype(bf16)
        for j in (2 * i, 2 * i + 1):
            if j < count:
                down_copies[j].start(priority=1)

    for copy in down_copies:
        copy.wait()
    down_started = []
    part_width = width // PARTS_DOWN
    for part in range(PARTS_DOWN):
        columns = slice(part * part_width, (part + 1) * part_width)
        product = None
        for i in range(count):
            term = jnp.dot(
                activated[:, starts[i] : starts[i] + sizes[i]],
                weights[i, 0 : sizes[i], columns],
                preferred_element_type=f32,
            )
            product = term if product is None else product + term
        to_partner(part, PARTS_DOWN, product, down_near, down_sems)
        if part > 0:
            down_started.append(to_owners(part - 1, PARTS_DOWN, down_near, down_far, down_sems))
    down_started.append(to_owners(PARTS_DOWN - 1, PARTS_DOWN, down_near, down_far, down_sems))
    for part in range(PARTS_DOWN):
        rows = pieces // PARTS_DOWN
        here = pl.ds(part * rows, rows)
        total = add_sums(part, PARTS_DOWN, down_started[part], down_far)
        stream[here] = stream[here] + total
    for c in range(pieces):
        layer_out[:, c * LANES : (c + 1) * LANES] = stream[c : c + 1, :].astype(bf16)

    features_sent()
    inputs_sent()
    for started in out_started + down_started:
        started[1]()
    for part in range(PARTS_OUT):
        pair_copy(part, out_near, out_sems).wait_send()
    for part in range(PARTS_DOWN):
        pair_copy(part, down_near, down_sems).wait_send()

    @pl.loop(0, pairs)
    def _(step):
        relay(step, me).wait_send()


def fused_layer(n, *operands):
    (
        residual,
        _,
        _,
        _,
        key_cache,
        _,
        _,
        keep_inputs,
        keep_hidden,
        norm_gain,
        out_weight,
        gate_weight,
        _,
        _,
    ) = operands
    width = residual.shape[1]
    pieces = width // LANES
    hidden = gate_weight.shape[0]
    count = -(-hidden // CHUNK)
    slots = 2 * count
    bf16, f32 = jnp.bfloat16, jnp.float32
    dma = pltpu.SemaphoreType.DMA
    vmem = pl.BlockSpec(memory_space=pltpu.VMEM)
    smem = pl.BlockSpec(memory_space=pltpu.SMEM)
    hbm = pl.BlockSpec(memory_space=pl.ANY)
    operands = list(operands)
    operands[9] = norm_gain.reshape(pieces, LANES)
    cache_shape = key_cache.shape[1:]
    row_shape = jax.ShapeDtypeStruct(residual.shape, bf16)
    weight_bytes = 2 * (out_weight.size + 3 * gate_weight.size)
    return pl.pallas_call(
        functools.partial(layer_kernel, n),
        out_shape=(row_shape, row_shape),
        in_specs=[vmem] * 4 + [hbm] * 2 + [smem] + [vmem] * 3 + [hbm] * 4,
        out_specs=(vmem, vmem),
        scratch_shapes=[
            pltpu.VMEM(cache_shape, bf16),
            pltpu.VMEM(cache_shape, bf16),
            pltpu.VMEM((slots, CHUNK, width), bf16),
            pltpu.VMEM((pieces, LANES), f32),
            pltpu.VMEM((pieces, LANES), f32),
            pltpu.VMEM((n, H // n, LANES), f32),
            pltpu.VMEM((n, H // n, LANES), f32),
            pltpu.VMEM((n, pieces, LANES), f32),
            pltpu.VMEM((pieces, LANES), f32),
            pltpu.VMEM((2, PARTS_OUT, n // 2, pieces // PARTS_OUT, LANES), bf16),
            pltpu.VMEM((2, PARTS_OUT, n // 2, pieces // PARTS_OUT, LANES), bf16),
            pltpu.VMEM((2, PARTS_DOWN, n // 2, pieces // PARTS_DOWN, LANES), bf16),
            pltpu.VMEM((2, PARTS_DOWN, n // 2, pieces // PARTS_DOWN, LANES), bf16),
            pltpu.VMEM((n, pieces, LANES), bf16),
            pltpu.VMEM((n, width), bf16),
            pltpu.VMEM((n, hidden), bf16),
            pltpu.VMEM((n, hidden), f32),
            dma((2,)),
            dma((out_weight.shape[0] // CHUNK + 3 * count,)),
            dma((n,)),
            dma((n,)),
            dma((PARTS_OUT, n // 2)),
            dma((PARTS_OUT, n // 2)),
            dma((n // 2,)),
            dma((n // 2,)),
            dma((n // 2,)),
            dma((n // 2,)),
            dma((PARTS_DOWN, n // 2)),
            dma((PARTS_DOWN, n // 2)),
        ],
        compiler_params=pltpu.CompilerParams(
            collective_id=0, has_side_effects=True, vmem_limit_bytes=63 * 2**20
        ),
        cost_estimate=pl.CostEstimate(
            flops=n * weight_bytes, bytes_accessed=weight_bytes, transcendentals=0
        ),
        name="layer",
    )(*operands)


def one_row_each(n, *operands):
    residual, gate_weight, out_weight = operands[0], operands[11], operands[10]
    slots = 2 * -(-gate_weight.shape[0] // CHUNK)
    return (
        residual.shape[0] == 1
        and n % 16 == 0
        and (H // KVH) % max(H // n, 1) == 0
        and out_weight.shape[0] == (H // n) * LANES
        and out_weight.shape[0] == 2 * CHUNK
        and 2 < slots <= MAX_SLOTS
        and gate_weight.shape[0] % 64 == 0
    )


def layer(n, *operands):
    if one_row_each(n, *operands):
        return fused_layer(n, *operands)
    return shards(*operands)


def solution(mesh):
    in_specs = (
        P(("group", "dev"), None),
        P(("group", "dev"), None),
        P(("group", "dev"), None),
        P(("group", "dev"), None),
        P(("group", "dev"), None, None),
        P(("group", "dev"), None, None),
        P(("group", "dev")),
        P("group", None),
        P("group", None),
        P(),
        P("dev", None),
        P("dev", None),
        P("dev", None),
        P("dev", None),
    )
    out_specs = (P(("group", "dev"), None), P(("group", "dev"), None))
    body = functools.partial(layer, mesh.shape["dev"])
    return jax.shard_map(body, mesh=mesh, in_specs=in_specs, out_specs=out_specs, check_vma=False)
```
